32 devices in a mesh: dp: 4 (over y, core), ctx: 8 (over z, x).
Axes of the slice: x: 2, y: 2, z: 4, core: 2. Of those that a mesh axis runs over, the one named last changes fastest.
Arguments:
- feat_clean: bfloat16 [4, 512, 6144], P('dp', 'ctx'), may hold values from -6 to 6
- feat_pert: bfloat16 [4, 512, 6144], P('dp', 'ctx'), may hold values from -6 to 6
- feat_teacher: bfloat16 [4, 512, 6144], P('dp', 'ctx'), may hold values from -6 to 6
- short_taps: float32 [3, 6144], replicated, may hold values from -3 to 3
- residues: float32 [2048, 16], replicated, may hold values from -0.26565564 to 0.26565564
- decay_rate: float32 [2048, 16], replicated, may hold values from 0.0001953125 to 0.0333333333
- out_weight: bfloat16 [2048, 4096], P(None, 'dp'), may hold values from -0.125 to 0.125
- norm_gain: float32 [4096], replicated, may hold values from 0.1 to 1.9
Outputs:
- grad_clean: bfloat16 [4, 512, 6144], P('dp', 'ctx')
- grad_pert: bfloat16 [4, 512, 6144], P('dp', 'ctx')
The draws below stay inside these ranges and needn't reach their ends.
All inputs are finite; a program needn't handle non-finite values.
Results may differ from the reference program's by a relative error of at most 0.018.
Values may be sent and summed in bfloat16 or wider, within the bound.
A program may use at most 192 MiB of HBM per device.

```python
import jax
import jax.numpy as jnp
from jax import lax

D = 4096
C = 2048
M = 16
LENGTH = 512
SEQS = 4


def mode_tables(key):
    first, second = jax.random.split(jax.random.fold_in(key, 7), 2)
    low = jnp.log(0.5 / LENGTH)
    high = jnp.log(1.0 / 30.0)
    rate = jnp.exp(low + (high - low) * jax.random.uniform(first, (C, M), jnp.float32))
    spread = jnp.clip(jax.random.normal(second, (C, M), jnp.float32), -4.0, 4.0)
    residue = spread * jnp.sqrt((2.0 * rate + 2.0 / LENGTH) / M)
    return (rate, residue)


def draw_decay_rate(key, part):
    return mode_tables(key)[0].astype(jnp.float32)


def draw_residues(key, part):
    return mode_tables(key)[1].astype(jnp.float32)


def block_scale(key, extent, pieces, smallest, top_value):
    factor_of, own = 1.0, jax.random.fold_in(key, 6)
    for axis_at, parts in pieces:
        heights = jnp.exp(jax.random.uniform(jax.random.fold_in(own, axis_at), (parts,), jnp.float32, smallest / len(pieces), top_value / len(pieces)))
        factor_of = factor_of * jnp.repeat(heights, extent[axis_at] // parts).reshape([-1 if axis == axis_at else 1 for axis in range(len(extent))])
    return factor_of


def noise(stream_key, shape, scale, limit, pieces=(), held_as=jnp.bfloat16):
    values = scale * jax.random.normal(stream_key, shape, jnp.float32)
    if pieces:
        values = values * block_scale(stream_key, shape, pieces, -0.22, 0.18)
    return jnp.clip(values, -limit, limit).astype(held_as)


def setup_inputs(seed: int = 0) -> dict:
    arg_keys = jax.random.split(jax.random.key(seed), 9)
    feat_clean = noise(arg_keys[0], (SEQS, LENGTH, 3 * C), 1.0, 6.0, ((0, 4), (1, 8)))
    feat_pert = noise(arg_keys[1], (SEQS, LENGTH, 3 * C), 1.0, 6.0, ((0, 4), (1, 8)))
    feat_teacher = noise(arg_keys[2], (SEQS, LENGTH, 3 * C), 1.0, 6.0, ((0, 4), (1, 8)))
    short_taps = noise(arg_keys[3], (3, 3 * C), 0.6, 3.0, (), jnp.float32)
    residues = draw_residues(jax.random.fold_in(arg_keys[8], 71), 0)
    decay_rate = draw_decay_rate(jax.random.fold_in(arg_keys[8], 71), 0)
    out_weight = noise(arg_keys[6], (C, D), C ** -0.5, 0.125, ((1, 4),))
    norm_gain = jnp.clip(1.0 + 0.18 * jax.random.normal(arg_keys[7], (D,), jnp.float32), 0.1, 1.9)
    return dict(feat_clean=feat_clean, feat_pert=feat_pert, feat_teacher=feat_teacher, short_taps=short_taps, residues=residues, decay_rate=decay_rate, out_weight=out_weight, norm_gain=norm_gain)


eps = 1e-06
teacher_weight = 0.5

def short_filter(features, taps):
    padded = jnp.pad(features.astype(jnp.float32), ((0, 0), (2, 0), (0, 0)))
    return taps[0] * padded[:, 2:] + taps[1] * padded[:, 1:-1] + taps[2] * padded[:, :-2]

def filter_spectrum(residues, decay_rate, length):
    positions = jnp.arange(length).astype(residues.dtype)
    kernel = jnp.zeros((residues.shape[0], length), residues.dtype)
    for mode in range(residues.shape[1]):
        kernel = kernel + residues[:, mode, None] * jnp.exp(-decay_rate[:, mode, None] * positions[None, :])
    return jnp.fft.rfft(kernel, n=2 * length, axis=-1)

def causal_conv(signal, spectrum):
    length = signal.shape[-1]
    full = jnp.fft.irfft(jnp.fft.rfft(signal, n=2 * length, axis=-1) * spectrum, n=2 * length, axis=-1)
    return full[..., :length]

def loss_slopes(mixer_outputs, squares, gain, full_width):
    inv_scale = lax.rsqrt(squares / full_width + eps)[..., None]
    normed = mixer_outputs * inv_scale * gain
    change = normed[:, 1] - normed[:, 0]
    clean_slope = -2.0 * change
    pert_slope = 2.0 * change + 2.0 * teacher_weight * (normed[:, 1] - normed[:, 2])
    return (jnp.stack([clean_slope, pert_slope], 1), inv_scale[:, :2])

def out_slopes(mixer_outputs, norm_slope, inv_scale, inner_sum, gain, full_width):
    value = inv_scale * gain * norm_slope - mixer_outputs[:, :2] * inv_scale ** 3 * (inner_sum / full_width)[..., None]
    return value.astype(jnp.bfloat16)

def reference(feat_clean, feat_pert, feat_teacher, short_taps, residues, decay_rate, out_weight, norm_gain):
    length = feat_clean.shape[1]
    spectrum = filter_spectrum(residues, decay_rate, length)
    mixing_weight = out_weight.astype(jnp.float32)
    full_width = norm_gain.shape[0]

    def one_sequence(group):
        features = jnp.stack([group[0], group[1], group[2]])
        mixed = short_filter(features, short_taps)
        width = mixed.shape[2] // 3
        key_part = mixed[..., width:2 * width]
        value_part = mixed[..., 2 * width:]
        query = mixed[..., :width].astype(jnp.bfloat16)
        gated = (key_part * value_part).astype(jnp.bfloat16)
        conv = causal_conv(jnp.swapaxes(gated, 1, 2).astype(jnp.float32), spectrum).astype(jnp.bfloat16)
        convolved_rows = jnp.swapaxes(conv, 1, 2)
        gated_product = (query.astype(jnp.float32) * convolved_rows.astype(jnp.float32)).astype(jnp.bfloat16)
        mixer_outputs = jnp.einsum('ivq,qp->ivp', gated_product.astype(jnp.float32), mixing_weight)[None]
        squares = lax.optimization_barrier(jnp.sum(mixer_outputs * mixer_outputs, -1))
        norm_slope, inv_scale = loss_slopes(mixer_outputs, squares, norm_gain, full_width)
        inner_sum = lax.optimization_barrier(jnp.sum(norm_gain * norm_slope * mixer_outputs[:, :2], -1))
        output_gradient = out_slopes(mixer_outputs, norm_slope, inv_scale, inner_sum, norm_gain, full_width)
        product_gradient = jnp.einsum('khe,ie->khi', output_gradient[0].astype(jnp.float32), mixing_weight)
        conv_slope = (product_gradient * query[:2].astype(jnp.float32)).astype(jnp.bfloat16)
        query_slope = product_gradient * convolved_rows[:2].astype(jnp.float32)
        flipped = jnp.flip(jnp.swapaxes(conv_slope, 1, 2).astype(jnp.float32), -1)
        gated_slope = jnp.flip(causal_conv(flipped, spectrum), -1).astype(jnp.bfloat16)
        gated_rows = jnp.swapaxes(gated_slope, 1, 2).astype(jnp.float32)
        unit_slope = jnp.concatenate([query_slope, gated_rows * value_part[:2], gated_rows * key_part[:2]], -1)
        padded = jnp.pad(unit_slope, ((0, 0), (0, 2), (0, 0)))
        feature_slope = short_taps[0] * padded[:, :-2] + short_taps[1] * padded[:, 1:-1] + short_taps[2] * padded[:, 2:]
        result = feature_slope.astype(jnp.bfloat16)
        return (result[0], result[1])
    grad_clean, grad_pert = lax.map(one_sequence, (feat_clean, feat_pert, feat_teacher))
    return (grad_clean, grad_pert)
```

```python
import math

import jax
import jax.numpy as jnp
from jax import lax
from jax.experimental import pallas as pl
from jax.experimental.pallas import tpu as pltpu
from jax.sharding import PartitionSpec as P

eps = 1e-06
teacher_weight = 0.5
f32 = jnp.float32
bf16 = jnp.bfloat16
LANES = 128
SUB = 8


def row_index():
    return lax.broadcasted_iota(jnp.int32, (SUB, LANES), 0).astype(f32)


def split_rows(value):
    return [value[SUB * i : SUB * (i + 1)] for i in range(value.shape[0] // SUB)]


def shifted_down(value, steps):
    if steps == 0:
        return value
    rows = lax.broadcasted_iota(jnp.int32, value.shape, 0)
    return jnp.where(rows >= steps, pltpu.roll(value, steps, 0), 0.0)


def shifted_up(value, steps):
    if steps == 0:
        return value
    count = value.shape[0]
    rows = lax.broadcasted_iota(jnp.int32, value.shape, 0)
    return jnp.where(rows < count - steps, pltpu.roll(value, count - steps, 0), 0.0)


def filter_table(res, rate, rows):
    row = row_index()
    tiles = [jnp.zeros((SUB, LANES), f32) for _ in range(rows // SUB)]
    for m in range(res.shape[0]):
        current = res[m : m + 1] * jnp.exp(-rate[m : m + 1] * row)
        step = jnp.exp(-rate[m : m + 1] * SUB)
        for i in range(len(tiles)):
            tiles[i] = tiles[i] + current
            current = current * step
    return jnp.concatenate(tiles, 0)


def direct_conv(value, table_row, causal):
    count = value.shape[0] // SUB
    out = [jnp.zeros((SUB, LANES), f32) for _ in range(count)]
    for b in range(SUB):
        tiles = split_rows(shifted_down(value, b) if causal else shifted_up(value, b))
        for a in range(count):
            weight = jnp.broadcast_to(table_row(SUB * a + b), (SUB, LANES))
            for i in range(count - a):
                if causal:
                    out[i + a] = out[i + a] + weight * tiles[i]
                else:
                    out[i] = out[i] + weight * tiles[i + a]
    return jnp.concatenate(out, 0)


def block_states(values, rate, causal, store):
    row = row_index()
    split = [split_rows(value) for value in values]
    count = len(split[0])
    for m in range(rate.shape[0]):
        one = rate[m : m + 1]
        step = jnp.exp(-one * SUB)
        if causal:
            current, order = jnp.exp(-one * (SUB - 1.0 - row)), range(count - 1, -1, -1)
        else:
            current, order = jnp.exp(-one * row), range(count)
        sums = [jnp.zeros((SUB, LANES), f32) for _ in split]
        for place, i in enumerate(order):
            sums = [total + current * tiles[i] for total, tiles in zip(sums, split)]
            if place < count - 1:
                current = current * step
        for s, total in enumerate(sums):
            store(s, m, jnp.sum(total, 0, keepdims=True))


def reached(locals_, state_row, res, rate, causal):
    row = row_index()
    split = [split_rows(value) for value in locals_]
    count = len(split[0])
    for m in range(rate.shape[0]):
        one = rate[m : m + 1]
        step = jnp.exp(-one * SUB)
        if causal:
            current, order = res[m : m + 1] * jnp.exp(-one * (row + 1.0)), range(count)
        else:
            current, order = res[m : m + 1] * jnp.exp(-one * (SUB - row)), range(count - 1, -1, -1)
        states = [jnp.broadcast_to(state_row(s, m), (SUB, LANES)) for s in range(len(split))]
        for place, i in enumerate(order):
            for s, tiles in enumerate(split):
                tiles[i] = tiles[i] + current * states[s]
            if place < count - 1:
                current = current * step
    return [jnp.concatenate(tiles, 0) for tiles in split]


def lane_loop(width, body):
    def step(i, carry):
        body(pl.ds(pl.multiple_of(i * LANES, LANES), LANES))
        return carry

    lax.fori_loop(0, width // LANES, step, 0)


def dp_peers():
    me = lax.axis_index("dp")
    chip, core = me // 2, me % 2
    sibling = chip * 2 + (1 - core)
    across = (1 - chip) * 2 + core
    diagonal = (1 - chip) * 2 + (1 - core)
    return me, sibling, across, diagonal


def mixer_kernel(
    prod_ref,
    weight_ref,
    gain_ref,
    slope_ref,
    rows_ref,
    y_ref,
    tile_ref,
    sums_ref,
    out_ref,
    hold_ref,
    send_ref,
    land_ref,
    send_sem,
    recv_sem,
    sum_send,
    sum_recv,
    back_send,
    back_recv,
):
    _, rows, width = prod_ref.shape
    own_width = weight_ref.shape[1]
    full_width = own_width * lax.axis_size("dp")
    me, sibling, across, diagonal = dp_peers()

    barrier = pltpu.get_barrier_semaphore()
    for peer in (sibling, across, diagonal):
        pl.semaphore_signal(
            barrier, inc=1, device_id={"dp": peer}, device_id_type=pl.DeviceIdType.MESH
        )
    pl.semaphore_wait(barrier, 3)

    def copy(source, target, send, recv, peer):
        return pltpu.make_async_remote_copy(
            src_ref=source,
            dst_ref=target,
            send_sem=send,
            recv_sem=recv,
            device_id={"dp": peer},
            device_id_type=pl.DeviceIdType.MESH,
        )

    forward = {}
    for s in range(3):
        for slot, peer in ((1, across), (0, sibling)):
            span = pl.ds(s * rows, rows)
            forward[slot, s] = copy(
                prod_ref.at[s],
                rows_ref.at[slot, span],
                send_sem.at[slot, s],
                recv_sem.at[slot, s],
                peer,
            )
            forward[slot, s].start()

    tile = min(256, own_width)

    def project(source, place):
        def step(i, carry):
            lanes = pl.ds(pl.multiple_of(i * tile, tile), tile)
            y_ref[place, :, lanes] = jnp.dot(
                source(), weight_ref[:, lanes], preferred_element_type=f32
            )
            return carry

        lax.fori_loop(0, own_width // tile, step, 0)

    def add_up(place):
        lane = lax.broadcasted_iota(jnp.int32, (SUB, LANES), 1)

        def step(i, carry):
            first = pl.multiple_of(i * SUB, SUB)
            yc, yp, yt = [y_ref[place, pl.ds(first + s * rows, SUB), :] for s in range(3)]
            gc, gp, gt = [gain_ref[...] * y for y in (yc, yp, yt)]
            pairs = ((yc, yc), (yp, yp), (yt, yt), (gc, gc), (gp, gp), (gc, gp), (gp, gt))
            result = jnp.zeros((SUB, LANES), f32)
            for n, (a, b) in enumerate(pairs):
                result = jnp.where(lane == n, jnp.sum(a * b, 1, keepdims=True), result)
            tile_ref[pl.ds(pl.multiple_of(place * rows + first, SUB), SUB), :] = result
            return carry

        lax.fori_loop(0, rows // SUB, step, 0)

    project(lambda: prod_ref[...].reshape(3 * rows, width), 0)
    add_up(0)
    for s in range(3):
        forward[1, s].wait_recv()
        span = pl.ds(s * rows, rows)
        forward[2, s] = copy(
            rows_ref.at[1, span],
            rows_ref.at[2, span],
            send_sem.at[2, s],
            recv_sem.at[2, s],
            sibling,
        )
        forward[2, s].start()
    for s in range(3):
        forward[0, s].wait_recv()
    project(lambda: rows_ref[0], 1)
    add_up(1)
    project(lambda: rows_ref[1], 2)
    add_up(2)
    for s in range(3):
        forward[2, s].wait_recv()
    project(lambda: rows_ref[2], 3)
    add_up(3)
    for s in range(3):
        for slot in range(3):
            forward[slot, s].wait_send()

    packed = tile_ref[...].T[:SUB]
    owners = (me, sibling, across, diagonal)
    for place, owner in enumerate(owners):
        sums_ref[me, owner] = packed[:, place * rows : (place + 1) * rows]
    exchanged = [
        copy(sums_ref.at[me], sums_ref.at[me], sum_send.at[n], sum_recv.at[n], peer)
        for n, peer in enumerate((sibling, across, diagonal))
    ]
    for one in exchanged:
        one.start()
    for one in exchanged:
        one.wait()
    total = sums_ref[0] + sums_ref[1] + sums_ref[2] + sums_ref[3]
    sums_ref[me] = total
    for place, owner in enumerate(owners):
        columns = jnp.concatenate(
            [sums_ref[me, owner], jnp.zeros((LANES - SUB, rows), f32)], 0
        )
        tile_ref[place * rows : (place + 1) * rows, :] = columns.T

    def slopes(place):
        high = 16

        def step(i, carry):
            first = pl.multiple_of(i * high, high)
            yc, yp, yt = [y_ref[place, pl.ds(first + s * rows, high), :] for s in range(3)]
            sums = tile_ref[pl.ds(pl.multiple_of(place * rows + first, high), high), :]
            inv_c, inv_p, inv_t = [
                lax.rsqrt(sums[:, n : n + 1] / full_width + eps) for n in range(3)
            ]
            cc, pp, cp, pt = [sums[:, n : n + 1] for n in range(3, 7)]
            inner_c = -2.0 * (inv_p * cp - inv_c * cc)
            inner_p = 2.0 * (inv_p * pp - inv_c * cp) + 2.0 * teacher_weight * (
                inv_p * pp - inv_t * pt
            )
            gain = gain_ref[...]
            nc, np_, nt = yc * inv_c * gain, yp * inv_p * gain, yt * inv_t * gain
            change = np_ - nc
            slope_c = -2.0 * change
            slope_p = 2.0 * change + 2.0 * teacher_weight * (np_ - nt)
            out_c = inv_c * gain * slope_c - yc * (inv_c * inv_c * inv_c * (inner_c / full_width))
            out_p = inv_p * gain * slope_p - yp * (inv_p * inv_p * inv_p * (inner_p / full_width))
            out_ref[place, pl.ds(first, high), :] = out_c.astype(bf16)
            out_ref[place, pl.ds(pl.multiple_of(rows + first, high), high), :] = out_p.astype(bf16)
            return carry

        lax.fori_loop(0, rows // high, step, 0)

    wide = min(256, width)

    def pull(place, store):
        def step(i, carry):
            lanes = pl.ds(pl.multiple_of(i * wide, wide), wide)
            store(
                lanes,
                lax.dot_general(
                    out_ref[place],
                    weight_ref[lanes, :],
                    (((1,), (1,)), ((), ())),
                    preferred_element_type=f32,
                ),
            )
            return carry

        lax.fori_loop(0, width // wide, step, 0)

    def to_send(slot):
        def store(lanes, value):
            send_ref[slot, :, lanes] = value.astype(bf16)

        return store

    def to_hold(lanes, value):
        hold_ref[:, lanes] = value

    backward = [
        copy(send_ref.at[n], land_ref.at[n], back_send.at[n], back_recv.at[n], peer)
        for n, peer in enumerate((sibling, across, sibling))
    ]
    slopes(3)
    pull(3, to_send(0))
    backward[0].start()
    slopes(2)
    pull(2, to_hold)
    backward[0].wait_recv()

    def join(i, carry):
        lanes = pl.ds(pl.multiple_of(i * wide, wide), wide)
        send_ref[1, :, lanes] = (hold_ref[:, lanes] + land_ref[0, :, lanes].astype(f32)).astype(bf16)
        return carry

    lax.fori_loop(0, width // wide, join, 0)
    backward[1].start()
    slopes(1)
    pull(1, to_send(2))
    backward[2].start()
    slopes(0)
    pull(0, to_hold)
    backward[2].wait_recv()
    backward[1].wait_recv()

    def finish(i, carry):
        lanes = pl.ds(pl.multiple_of(i * wide, wide), wide)
        total = (
            hold_ref[:, lanes]
            + land_ref[2, :, lanes].astype(f32)
            + land_ref[1, :, lanes].astype(f32)
        )
        slope_ref[0, :, lanes] = total[:rows]
        slope_ref[1, :, lanes] = total[rows:]
        return carry

    lax.fori_loop(0, width // wide, finish, 0)
    for one in backward:
        one.wait_send()


def mixer(prod, weight, gain):
    _, rows, width = prod.shape
    own_width = weight.shape[1]
    return pl.pallas_call(
        mixer_kernel,
        in_specs=[pl.BlockSpec(memory_space=pltpu.VMEM)] * 3,
        out_specs=pl.BlockSpec(memory_space=pltpu.VMEM),
        out_shape=jax.ShapeDtypeStruct((2, rows, width), f32),
        scratch_shapes=[
            pltpu.VMEM((3, 3 * rows, width), bf16),
            pltpu.VMEM((4, 3 * rows, own_width), f32),
            pltpu.VMEM((4 * rows, LANES), f32),
            pltpu.VMEM((4, 4, SUB, rows), f32),
            pltpu.VMEM((4, 2 * rows, own_width), bf16),
            pltpu.VMEM((2 * rows, width), f32),
            pltpu.VMEM((3, 2 * rows, width), bf16),
            pltpu.VMEM((3, 2 * rows, width), bf16),
            pltpu.SemaphoreType.DMA((3, 3)),
            pltpu.SemaphoreType.DMA((3, 3)),
            pltpu.SemaphoreType.DMA((3,)),
            pltpu.SemaphoreType.DMA((3,)),
            pltpu.SemaphoreType.DMA((3,)),
            pltpu.SemaphoreType.DMA((3,)),
        ],
        compiler_params=pltpu.CompilerParams(
            collective_id=0, has_side_effects=True, vmem_limit_bytes=56 * 2**20
        ),
        name="mixer",
    )(prod, weight, gain)


def ctx_line():
    me = lax.axis_index("ctx")
    count = lax.axis_size("ctx")
    return me, count, lax.rem(me + 1, count), lax.rem(me + count - 1, count)


def greet(peers):
    barrier = pltpu.get_barrier_semaphore()
    for peer in peers:
        pl.semaphore_signal(
            barrier, inc=1, device_id={"ctx": peer}, device_id_type=pl.DeviceIdType.MESH
        )
    pl.semaphore_wait(barrier, len(peers))


def ctx_copy(source, target, send, recv, peer):
    return pltpu.make_async_remote_copy(
        src_ref=source,
        dst_ref=target,
        send_sem=send,
        recv_sem=recv,
        device_id={"ctx": peer},
        device_id_type=pl.DeviceIdType.MESH,
    )


def carry_states(going_ref, coming_ref, rate_ref, rows, send_sem, recv_sem, peer, is_first, is_last):
    pieces = send_sem.shape[0]
    modes, width = rate_ref.shape
    streams = going_ref.shape[0]
    piece = width // pieces
    copies = [
        ctx_copy(
            going_ref.at[:, :, pl.ds(c * piece, piece)],
            coming_ref.at[:, :, pl.ds(c * piece, piece)],
            send_sem.at[c],
            recv_sem.at[c],
            peer,
        )
        for c in range(pieces)
    ]

    @pl.when(is_first)
    def _():
        coming_ref[...] = jnp.zeros(coming_ref.shape, f32)

    for c in range(pieces):

        @pl.when(jnp.logical_not(is_first))
        def _():
            copies[c].wait_recv()

        @pl.when(jnp.logical_not(is_last))
        def _():
            def step(i, carry):
                lanes = pl.ds(pl.multiple_of(c * piece + i * LANES, LANES), LANES)
                decay = jnp.exp(-rate_ref[:, lanes] * rows)
                for s in range(streams):
                    going_ref[s, :, lanes] = going_ref[s, :, lanes] + decay * coming_ref[s, :, lanes]
                return carry

            lax.fori_loop(0, piece // LANES, step, 0)
            copies[c].start()

    def settle():
        @pl.when(jnp.logical_not(is_last))
        def _():
            for one in copies:
                one.wait_send()

    return settle


def front_kernel(
    clean_ref,
    pert_ref,
    teacher_ref,
    tap_ref,
    res_ref,
    rate_ref,
    query_ref,
    key_ref,
    value_ref,
    conv_ref,
    prod_ref,
    table_ref,
    halo_out,
    halo_in,
    gated_ref,
    going_ref,
    coming_ref,
    halo_sem,
    send_sem,
    recv_sem,
):
    feats = (clean_ref, pert_ref, teacher_ref)
    rows, width = clean_ref.shape[1], clean_ref.shape[2] // 3
    me, count, after, before = ctx_line()
    is_first, is_last = me == 0, me == count - 1
    greet((after, before))

    def heads(lanes):
        tails = [f[0, rows - 16 :, lanes].astype(f32)[14:] for f in feats]
        halo_out[:, lanes] = jnp.concatenate(tails + [jnp.zeros((2, LANES), f32)], 0)

    lane_loop(3 * width, heads)
    halo = ctx_copy(halo_out, halo_in, halo_sem.at[0], halo_sem.at[1], after)

    @pl.when(jnp.logical_not(is_last))
    def _():
        halo.start()

    def tables(lanes):
        table_ref[:, lanes] = filter_table(res_ref[:, lanes], rate_ref[:, lanes], rows)

    lane_loop(width, tables)

    @pl.when(is_first)
    def _():
        halo_in[...] = jnp.zeros(halo_in.shape, f32)

    @pl.when(jnp.logical_not(is_first))
    def _():
        halo.wait_recv()

    row = lambda: lax.broadcasted_iota(jnp.int32, (rows, LANES), 0)

    def filtered(s, lanes):
        here = feats[s][0, :, lanes].astype(f32)
        back_two, back_one = halo_in[2 * s : 2 * s + 1, lanes], halo_in[2 * s + 1 : 2 * s + 2, lanes]
        one = jnp.where(row() >= 1, pltpu.roll(here, 1, 0), back_one)
        two = jnp.where(
            row() >= 2, pltpu.roll(here, 2, 0), jnp.where(row() == 1, back_one, back_two)
        )
        return (
            tap_ref[0:1, lanes] * here + tap_ref[1:2, lanes] * one + tap_ref[2:3, lanes] * two
        )

    def features(i, carry):
        lanes, klanes, vlanes = [
            pl.ds(pl.multiple_of(i * LANES + j * width, LANES), LANES) for j in range(3)
        ]
        gated = []
        for s in range(3):
            query_ref[s, :, lanes] = filtered(s, lanes).astype(bf16)
            k, v = filtered(s, klanes), filtered(s, vlanes)
            if s < 2:
                key_ref[s, :, lanes] = k
                value_ref[s, :, lanes] = v
            gated.append((k * v).astype(bf16).astype(f32))
            gated_ref[s, :, lanes] = gated[s]

        def store(s, m, value):
            going_ref[s, pl.ds(m, 1), lanes] = value

        block_states(gated, rate_ref[:, lanes], True, store)
        return carry

    lax.fori_loop(0, width // LANES, features, 0)

    def direct(lanes):
        for s in range(3):
            gated_ref[s, :, lanes] = direct_conv(
                gated_ref[s, :, lanes], lambda j: table_ref[pl.ds(j, 1), lanes], True
            )

    late = me >= count // 2

    @pl.when(late)
    def _():
        lane_loop(width, direct)

    settle = carry_states(
        going_ref, coming_ref, rate_ref, rows, send_sem, recv_sem, after, is_first, is_last
    )

    @pl.when(jnp.logical_not(late))
    def _():
        lane_loop(width, direct)

    def finish(lanes):
        full = reached(
            [gated_ref[s, :, lanes] for s in range(3)],
            lambda s, m: coming_ref[s, pl.ds(m, 1), lanes],
            res_ref[:, lanes],
            rate_ref[:, lanes],
            True,
        )
        for s in range(3):
            conv = full[s].astype(bf16)
            if s < 2:
                conv_ref[s, :, lanes] = conv
            prod_ref[s, :, lanes] = (
                query_ref[s, :, lanes].astype(f32) * conv.astype(f32)
            ).astype(bf16)

    lane_loop(width, finish)
    settle()

    @pl.when(jnp.logical_not(is_last))
    def _():
        halo.wait_send()


def pieces_of(width):
    return math.gcd(width // LANES, 4)


def front(feats, taps, res, rate):
    _, rows, width3 = feats[0].shape
    width, modes = width3 // 3, res.shape[0]
    pieces = pieces_of(width)
    vmem = pl.BlockSpec(memory_space=pltpu.VMEM)
    return pl.pallas_call(
        front_kernel,
        in_specs=[vmem] * 6,
        out_specs=[vmem] * 6,
        out_shape=[
            jax.ShapeDtypeStruct((3, rows, width), bf16),
            jax.ShapeDtypeStruct((2, rows, width), f32),
            jax.ShapeDtypeStruct((2, rows, width), f32),
            jax.ShapeDtypeStruct((2, rows, width), bf16),
            jax.ShapeDtypeStruct((3, rows, width), bf16),
            jax.ShapeDtypeStruct((rows, width), f32),
        ],
        scratch_shapes=[
            pltpu.VMEM((SUB, 3 * width), f32),
            pltpu.VMEM((SUB, 3 * width), f32),
            pltpu.VMEM((3, rows, width), f32),
            pltpu.VMEM((3, modes, width), f32),
            pltpu.VMEM((3, modes, width), f32),
            pltpu.SemaphoreType.DMA((2,)),
            pltpu.SemaphoreType.DMA((pieces,)),
            pltpu.SemaphoreType.DMA((pieces,)),
        ],
        compiler_params=pltpu.CompilerParams(
            collective_id=1, has_side_effects=True, vmem_limit_bytes=56 * 2**20
        ),
        name="front",
    )(*feats, taps, res, rate)


def back_kernel(
    slope_ref,
    query_ref,
    key_ref,
    value_ref,
    conv_ref,
    table_ref,
    tap_ref,
    res_ref,
    rate_ref,
    clean_ref,
    pert_ref,
    halo_out,
    halo_in,
    local_ref,
    tail_ref,
    going_ref,
    coming_ref,
    halo_sem,
    send_sem,
    recv_sem,
):
    grads = (clean_ref, pert_ref)
    _, rows, width = slope_ref.shape
    me, count, after, before = ctx_line()
    is_first, is_last = me == count - 1, me == 0
    greet((after, before))

    def slopes(lanes):
        values = [
            (slope_ref[s, :, lanes] * query_ref[s, :, lanes].astype(f32)).astype(bf16).astype(f32)
            for s in range(2)
        ]
        for s in range(2):
            local_ref[s, :, lanes] = values[s]

        def store(s, m, value):
            going_ref[s, pl.ds(m, 1), lanes] = value

        block_states(values, rate_ref[:, lanes], False, store)

    lane_loop(width, slopes)

    def direct(lanes):
        for s in range(2):
            local_ref[s, :, lanes] = direct_conv(
                local_ref[s, :, lanes], lambda j: table_ref[pl.ds(j, 1), lanes], False
            )

    late = me < count // 2

    @pl.when(late)
    def _():
        lane_loop(width, direct)

    settle = carry_states(
        going_ref, coming_ref, rate_ref, rows, send_sem, recv_sem, before, is_first, is_last
    )

    @pl.when(jnp.logical_not(late))
    def _():
        lane_loop(width, direct)

    def tapped(unit, lanes, next_one, next_two):
        high = unit.shape[0]
        row = lax.broadcasted_iota(jnp.int32, unit.shape, 0)
        one = jnp.where(row < high - 1, pltpu.roll(unit, high - 1, 0), next_one)
        two = jnp.where(
            row < high - 2,
            pltpu.roll(unit, high - 2, 0),
            jnp.where(row == high - 2, next_one, next_two),
        )
        return (
            tap_ref[0:1, lanes] * unit + tap_ref[1:2, lanes] * one + tap_ref[2:3, lanes] * two
        ).astype(bf16)

    def units(i, carry):
        places = [pl.ds(pl.multiple_of(i * LANES + j * width, LANES), LANES) for j in range(3)]
        lanes = places[0]
        full = reached(
            [local_ref[s, :, lanes] for s in range(2)],
            lambda s, m: coming_ref[s, pl.ds(m, 1), lanes],
            res_ref[:, lanes],
            rate_ref[:, lanes],
            False,
        )
        none = jnp.zeros((1, LANES), f32)
        for j, place in enumerate(places):
            firsts = []
            for s in range(2):
                if j == 0:
                    unit = slope_ref[s, :, lanes] * conv_ref[s, :, lanes].astype(f32)
                else:
                    other = value_ref if j == 1 else key_ref
                    unit = full[s].astype(bf16).astype(f32) * other[s, :, lanes]
                firsts.append(unit[:2])
                tail_ref[s, :, place] = unit[rows - 16 :]
                grads[s][0, :, place] = tapped(unit, place, none, none)
            halo_out[:, place] = jnp.concatenate(firsts + [jnp.zeros((4, LANES), f32)], 0)
        return carry

    lax.fori_loop(0, width // LANES, units, 0)
    halo = ctx_copy(halo_out, halo_in, halo_sem.at[0], halo_sem.at[1], before)

    @pl.when(jnp.logical_not(is_last))
    def _():
        halo.start()

    @pl.when(jnp.logical_not(is_first))
    def _():
        halo.wait_recv()

        def mend(lanes):
            for s in range(2):
                grads[s][0, rows - 16 :, lanes] = tapped(
                    tail_ref[s, :, lanes],
                    lanes,
                    halo_in[2 * s : 2 * s + 1, lanes],
                    halo_in[2 * s + 1 : 2 * s + 2, lanes],
                )

        lane_loop(3 * width, mend)

    settle()

    @pl.when(jnp.logical_not(is_last))
    def _():
        halo.wait_send()


def back(prod_slope, query, key_part, value_part, conv, table, taps, res, rate):
    _, rows, width = prod_slope.shape
    modes = res.shape[0]
    pieces = pieces_of(width)
    vmem = pl.BlockSpec(memory_space=pltpu.VMEM)
    return pl.pallas_call(
        back_kernel,
        in_specs=[vmem] * 9,
        out_specs=[vmem] * 2,
        out_shape=[jax.ShapeDtypeStruct((1, rows, 3 * width), bf16)] * 2,
        scratch_shapes=[
            pltpu.VMEM((SUB, 3 * width), f32),
            pltpu.VMEM((SUB, 3 * width), f32),
            pltpu.VMEM((2, rows, width), f32),
            pltpu.VMEM((2, 16, 3 * width), f32),
            pltpu.VMEM((2, modes, width), f32),
            pltpu.VMEM((2, modes, width), f32),
            pltpu.SemaphoreType.DMA((2,)),
            pltpu.SemaphoreType.DMA((pieces,)),
            pltpu.SemaphoreType.DMA((pieces,)),
        ],
        compiler_params=pltpu.CompilerParams(
            collective_id=2, has_side_effects=True, vmem_limit_bytes=56 * 2**20
        ),
        name="back",
    )(prod_slope, query, key_part, value_part, conv, table, taps, res, rate)


def per_device(
    feat_clean, feat_pert, feat_teacher, short_taps, residues, decay_rate, out_weight, norm_gain
):
    res, rate = residues.T, decay_rate.T
    query, key_part, value_part, conv, prod, table = front(
        (feat_clean, feat_pert, feat_teacher), short_taps, res, rate
    )
    own_width = out_weight.shape[1]
    gain = lax.dynamic_slice_in_dim(norm_gain, lax.axis_index("dp") * own_width, own_width, 0)
    prod_slope = mixer(prod, out_weight, gain[None])
    return back(prod_slope, query, key_part, value_part, conv, table, short_taps, res, rate)


def solution(mesh):
    in_specs = (
        P("dp", "ctx", None),
        P("dp", "ctx", None),
        P("dp", "ctx", None),
        P(),
        P(),
        P(),
        P(None, "dp"),
        P(),
    )
    out_specs = (P("dp", "ctx", None), P("dp", "ctx", None))
    return jax.shard_map(
        per_device, mesh=mesh, in_specs=in_specs, out_specs=out_specs, check_vma=False
    )
```

```python
import math

import jax
import jax.numpy as jnp
from jax import lax
from jax.experimental import pallas as pl
from jax.experimental.pallas import tpu as pltpu
from jax.sharding import PartitionSpec as P

eps = 1e-06
teacher_weight = 0.5
f32 = jnp.float32
bf16 = jnp.bfloat16
LANES = 128
SUB = 8


def row_index():
    return lax.broadcasted_iota(jnp.int32, (SUB, LANES), 0).astype(f32)


def split_rows(value):
    return [value[SUB * i : SUB * (i + 1)] for i in range(value.shape[0] // SUB)]


def shifted_down(value, steps):
    if steps == 0:
        return value
    rows = lax.broadcasted_iota(jnp.int32, value.shape, 0)
    return jnp.where(rows >= steps, pltpu.roll(value, steps, 0), 0.0)


def shifted_up(value, steps):
    if steps == 0:
        return value
    count = value.shape[0]
    rows = lax.broadcasted_iota(jnp.int32, value.shape, 0)
    return jnp.where(rows < count - steps, pltpu.roll(value, count - steps, 0), 0.0)


def filter_table(res, rate, rows):
    row = row_index()
    tiles = [jnp.zeros((SUB, LANES), f32) for _ in range(rows // SUB)]
    for m in range(res.shape[0]):
        current = res[m : m + 1] * jnp.exp(-rate[m : m + 1] * row)
        step = jnp.exp(-rate[m : m + 1] * SUB)
        for i in range(len(tiles)):
            tiles[i] = tiles[i] + current
            current = current * step
    return jnp.concatenate(tiles, 0)


def direct_conv(value, table_row, causal):
    count = value.shape[0] // SUB
    out = [jnp.zeros((SUB, LANES), f32) for _ in range(count)]
    for b in range(SUB):
        tiles = split_rows(shifted_down(value, b) if causal else shifted_up(value, b))
        for a in range(count):
            weight = jnp.broadcast_to(table_row(SUB * a + b), (SUB, LANES))
            for i in range(count - a):
                if causal:
                    out[i + a] = out[i + a] + weight * tiles[i]
                else:
                    out[i] = out[i] + weight * tiles[i + a]
    return jnp.concatenate(out, 0)


def block_states(values, rate, causal, store):
    row = row_index()
    split = [split_rows(value) for value in values]
    count = len(split[0])
    for m in range(rate.shape[0]):
        one = rate[m : m + 1]
        step = jnp.exp(-one * SUB)
        if causal:
            current, order = jnp.exp(-one * (SUB - 1.0 - row)), range(count - 1, -1, -1)
        else:
            current, order = jnp.exp(-one * row), range(count)
        sums = [jnp.zeros((SUB, LANES), f32) for _ in split]
        for place, i in enumerate(order):
            sums = [total + current * tiles[i] for total, tiles in zip(sums, split)]
            if place < count - 1:
                current = current * step
        for s, total in enumerate(sums):
            store(s, m, jnp.sum(total, 0, keepdims=True))


def reached(locals_, state_row, res, rate, causal):
    row = row_index()
    split = [split_rows(value) for value in locals_]
    count = len(split[0])
    for m in range(rate.shape[0]):
        one = rate[m : m + 1]
        step = jnp.exp(-one * SUB)
        if causal:
            current, order = res[m : m + 1] * jnp.exp(-one * (row + 1.0)), range(count)
        else:
            current, order = res[m : m + 1] * jnp.exp(-one * (SUB - row)), range(count - 1, -1, -1)
        states = [jnp.broadcast_to(state_row(s, m), (SUB, LANES)) for s in range(len(split))]
        for place, i in enumerate(order):
            for s, tiles in enumerate(split):
                tiles[i] = tiles[i] + current * states[s]
            if place < count - 1:
                current = current * step
    return [jnp.concatenate(tiles, 0) for tiles in split]


def lane_loop(width, body):
    def step(i, carry):
        body(pl.ds(pl.multiple_of(i * LANES, LANES), LANES))
        return carry

    lax.fori_loop(0, width // LANES, step, 0)


MESH = pl.DeviceIdType.MESH


def remote(axis, source, target, send, recv, peer):
    return pltpu.make_async_remote_copy(
        src_ref=source,
        dst_ref=target,
        send_sem=send,
        recv_sem=recv,
        device_id={axis: peer},
        device_id_type=MESH,
    )


def dp_peers():
    me = lax.axis_index("dp")
    chip, core = me // 2, me % 2
    sibling = chip * 2 + (1 - core)
    across = (1 - chip) * 2 + core
    diagonal = (1 - chip) * 2 + (1 - core)
    return me, sibling, across, diagonal


def mixer_grads_kernel(
    clean_ref,
    pert_ref,
    teacher_ref,
    tap_ref,
    res_ref,
    rate_ref,
    gain_ref,
    weight_hbm,
    grad_clean_ref,
    grad_pert_ref,
    weight_ref,
    query_ref,
    key_ref,
    value_ref,
    conv_ref,
    prod_ref,
    table_ref,
    gated_ref,
    slope_ref,
    local_ref,
    tail_ref,
    halo_out,
    halo_in,
    head_out,
    head_in,
    going_ref,
    coming_ref,
    back_going_ref,
    back_coming_ref,
    rows_ref,
    y_ref,
    tile_ref,
    sums_ref,
    out_ref,
    hold_ref,
    send_ref,
    land_ref,
    weight_sem,
    halo_sem,
    head_sem,
    chain_send,
    chain_recv,
    back_chain_send,
    back_chain_recv,
    row_send,
    row_recv,
    sum_send,
    sum_recv,
    part_send,
    part_recv,
):
    feats = (clean_ref, pert_ref, teacher_ref)
    grads = (grad_clean_ref, grad_pert_ref)
    rows, width = clean_ref.shape[1], clean_ref.shape[2] // 3
    own_width = weight_ref.shape[1]
    full_width = own_width * lax.axis_size("dp")
    pieces = part_send.shape[1]
    piece = width // pieces
    links = chain_send.shape[0]
    link = width // links
    links_each = links // pieces
    here, count = lax.axis_index("ctx"), lax.axis_size("ctx")
    after, before = lax.rem(here + 1, count), lax.rem(here + count - 1, count)
    at_start, at_end = here == 0, here == count - 1
    inside_start, inside_end = here > 0, here < count - 1
    upper = here >= count // 2
    lower = here < count // 2
    me, sibling, across, diagonal = dp_peers()

    def span_of(c):
        return pl.ds(c * piece, piece)

    def piece_loop(c, body):
        def step(i, carry):
            body(pl.multiple_of(c * piece + i * LANES, LANES))
            return carry

        lax.fori_loop(0, piece // LANES, step, 0)

    def lanes_at(first):
        return pl.ds(pl.multiple_of(first, LANES), LANES)

    weight_copy = pltpu.make_async_copy(weight_hbm, weight_ref, weight_sem.at[0])
    weight_copy.start()

    barrier = pltpu.get_barrier_semaphore()
    for peer in (after, before):
        pl.semaphore_signal(barrier, inc=1, device_id={"ctx": peer}, device_id_type=MESH)
    for peer in (sibling, across, diagonal):
        pl.semaphore_signal(barrier, inc=1, device_id={"dp": peer}, device_id_type=MESH)

    def tails(lanes):
        kept = [f[0, rows - 16 :, lanes].astype(f32)[14:] for f in feats]
        halo_out[:, lanes] = jnp.concatenate(kept + [jnp.zeros((2, LANES), f32)], 0)

    lane_loop(3 * width, tails)
    pl.semaphore_wait(barrier, 5)
    halo = remote("ctx", halo_out, halo_in, halo_sem.at[0], halo_sem.at[1], after)

    @pl.when(inside_end)
    def _():
        halo.start()

    def tables(lanes):
        table_ref[:, lanes] = filter_table(res_ref[:, lanes], rate_ref[:, lanes], rows)

    lane_loop(width, tables)

    @pl.when(at_start)
    def _():
        halo_in[...] = jnp.zeros(halo_in.shape, f32)

    @pl.when(inside_start)
    def _():
        halo.wait_recv()

    def filtered(s, lanes):
        row = lax.broadcasted_iota(jnp.int32, (rows, LANES), 0)
        now = feats[s][0, :, lanes].astype(f32)
        back_two, back_one = halo_in[2 * s : 2 * s + 1, lanes], halo_in[2 * s + 1 : 2 * s + 2, lanes]
        one = jnp.where(row >= 1, pltpu.roll(now, 1, 0), back_one)
        two = jnp.where(row >= 2, pltpu.roll(now, 2, 0), jnp.where(row == 1, back_one, back_two))
        return tap_ref[0:1, lanes] * now + tap_ref[1:2, lanes] * one + tap_ref[2:3, lanes] * two

    def features(first):
        lanes, klanes, vlanes = [lanes_at(first + j * width) for j in range(3)]
        gated = []
        for s in range(3):
            query_ref[s, :, lanes] = filtered(s, lanes).astype(bf16)
            k, v = filtered(s, klanes), filtered(s, vlanes)
            if s < 2:
                key_ref[s, :, lanes] = k
                value_ref[s, :, lanes] = v
            gated.append((k * v).astype(bf16).astype(f32))
            gated_ref[s, :, lanes] = gated[s]

        def store(s, m, value):
            going_ref[s, pl.ds(m, 1), lanes] = value

        block_states(gated, rate_ref[:, lanes], True, store)

    def link_of(c):
        return pl.ds(c * link, link)

    def pass_on(c, going, coming, copies, is_first, inside_first, inside_last):
        @pl.when(is_first)
        def _():
            coming[:, :, link_of(c)] = jnp.zeros((coming.shape[0], coming.shape[1], link), f32)

        @pl.when(inside_first)
        def _():
            copies[c].wait_recv()

        @pl.when(inside_last)
        def _():
            lanes = link_of(c)
            decay = jnp.exp(-rate_ref[:, lanes] * rows)
            for s in range(going.shape[0]):
                going[s, :, lanes] = going[s, :, lanes] + decay * coming[s, :, lanes]
            copies[c].start()

    def chain(going, coming, send, recv, peer):
        return [
            remote(
                "ctx",
                going.at[:, :, link_of(c)],
                coming.at[:, :, link_of(c)],
                send.at[c],
                recv.at[c],
                peer,
            )
            for c in range(links)
        ]

    forward_chain = chain(going_ref, coming_ref, chain_send, chain_recv, after)
    backward_chain = chain(back_going_ref, back_coming_ref, back_chain_send, back_chain_recv, before)

    def direct(first):
        lanes = lanes_at(first)
        for s in range(3):
            gated_ref[s, :, lanes] = direct_conv(
                gated_ref[s, :, lanes], lambda j: table_ref[pl.ds(j, 1), lanes], True
            )

    def finish(first):
        lanes = lanes_at(first)
        full = reached(
            [gated_ref[s, :, lanes] for s in range(3)],
            lambda s, m: coming_ref[s, pl.ds(m, 1), lanes],
            res_ref[:, lanes],
            rate_ref[:, lanes],
            True,
        )
        for s in range(3):
            conv = full[s].astype(bf16)
            if s < 2:
                conv_ref[s, :, lanes] = conv
            prod_ref[s * rows : (s + 1) * rows, lanes] = (
                query_ref[s, :, lanes].astype(f32) * conv.astype(f32)
            ).astype(bf16)

    def row_copy(slot, c):
        source = rows_ref.at[1] if slot == 2 else prod_ref
        return remote(
            "dp",
            source.at[:, span_of(c)],
            rows_ref.at[slot, :, span_of(c)],
            row_send.at[slot, c],
            row_recv.at[slot, c],
            across if slot == 1 else sibling,
        )

    row_copies = [[row_copy(slot, c) for c in range(pieces)] for slot in range(3)]

    def forward_pass(c):
        for n in range(c * links_each, (c + 1) * links_each):
            pass_on(n, going_ref, coming_ref, forward_chain, at_start, inside_start, inside_end)

    for c in range(pieces):
        piece_loop(c, features)

    @pl.when(upper)
    def _():
        for c in range(pieces):
            piece_loop(c, direct)
        for c in range(pieces):
            forward_pass(c)
            piece_loop(c, finish)
            row_copies[1][c].start()
            row_copies[0][c].start()

    @pl.when(lower)
    def _():
        for c in range(pieces):
            forward_pass(c)
        for c in range(pieces):
            piece_loop(c, direct)
            piece_loop(c, finish)
            row_copies[1][c].start()
            row_copies[0][c].start()

    weight_copy.wait()
    tile = min(256, own_width)

    def project(source, place, c):
        def step(i, carry):
            lanes = pl.ds(pl.multiple_of(i * tile, tile), tile)
            part = jnp.dot(source(), weight_ref[span_of(c), lanes], preferred_element_type=f32)
            y_ref[place, :, lanes] = part if c == 0 else y_ref[place, :, lanes] + part
            return carry

        lax.fori_loop(0, own_width // tile, step, 0)

    def add_up(place):
        lane = lax.broadcasted_iota(jnp.int32, (SUB, LANES), 1)

        def step(i, carry):
            first = pl.multiple_of(i * SUB, SUB)
            yc, yp, yt = [y_ref[place, pl.ds(first + s * rows, SUB), :] for s in range(3)]
            gc, gp, gt = [gain_ref[...] * y for y in (yc, yp, yt)]
            pairs = ((yc, yc), (yp, yp), (yt, yt), (gc, gc), (gp, gp), (gc, gp), (gp, gt))
            result = jnp.zeros((SUB, LANES), f32)
            for n, (a, b) in enumerate(pairs):
                result = jnp.where(lane == n, jnp.sum(a * b, 1, keepdims=True), result)
            tile_ref[pl.ds(pl.multiple_of(place * rows + first, SUB), SUB), :] = result
            return carry

        lax.fori_loop(0, rows // SUB, step, 0)

    for c in range(pieces):
        project(lambda: prod_ref[:, span_of(c)], 0, c)
    add_up(0)
    for c in range(pieces):
        row_copies[1][c].wait_recv()
        row_copies[2][c].start()
        row_copies[0][c].wait_recv()
        project(lambda: rows_ref[0, :, span_of(c)], 1, c)
        project(lambda: rows_ref[1, :, span_of(c)], 2, c)
        if c > 0:
            row_copies[2][c - 1].wait_recv()
            project(lambda: rows_ref[2, :, span_of(c - 1)], 3, c - 1)
    add_up(1)
    add_up(2)
    row_copies[2][pieces - 1].wait_recv()
    project(lambda: rows_ref[2, :, span_of(pieces - 1)], 3, pieces - 1)
    add_up(3)

    packed = tile_ref[...].T[:SUB]
    owners = (me, sibling, across, diagonal)
    for place, owner in enumerate(owners):
        sums_ref[me, owner] = packed[:, place * rows : (place + 1) * rows]
    exchanged = [
        remote("dp", sums_ref.at[me], sums_ref.at[me], sum_send.at[n], sum_recv.at[n], peer)
        for n, peer in enumerate((sibling, across, diagonal))
    ]
    for one in exchanged:
        one.start()
    for one in exchanged:
        one.wait()
    sums_ref[me] = sums_ref[0] + sums_ref[1] + sums_ref[2] + sums_ref[3]
    for place, owner in enumerate(owners):
        columns = jnp.concatenate([sums_ref[me, owner], jnp.zeros((LANES - SUB, rows), f32)], 0)
        tile_ref[place * rows : (place + 1) * rows, :] = columns.T

    def slopes(place):
        high = 16

        def step(i, carry):
            first = pl.multiple_of(i * high, high)
            yc, yp, yt = [y_ref[place, pl.ds(first + s * rows, high), :] for s in range(3)]
            sums = tile_ref[pl.ds(pl.multiple_of(place * rows + first, high), high), :]
            inv_c, inv_p, inv_t = [
                lax.rsqrt(sums[:, n : n + 1] / full_width + eps) for n in range(3)
            ]
            cc, pp, cp, pt = [sums[:, n : n + 1] for n in range(3, 7)]
            inner_c = -2.0 * (inv_p * cp - inv_c * cc)
            inner_p = 2.0 * (inv_p * pp - inv_c * cp) + 2.0 * teacher_weight * (
                inv_p * pp - inv_t * pt
            )
            gain = gain_ref[...]
            nc, np_, nt = yc * inv_c * gain, yp * inv_p * gain, yt * inv_t * gain
            change = np_ - nc
            slope_c = -2.0 * change
            slope_p = 2.0 * change + 2.0 * teacher_weight * (np_ - nt)
            out_c = inv_c * gain * slope_c - yc * (inv_c * inv_c * inv_c * (inner_c / full_width))
            out_p = inv_p * gain * slope_p - yp * (inv_p * inv_p * inv_p * (inner_p / full_width))
            out_ref[place, pl.ds(first, high), :] = out_c.astype(bf16)
            out_ref[place, pl.ds(pl.multiple_of(rows + first, high), high), :] = out_p.astype(bf16)
            return carry

        lax.fori_loop(0, rows // high, step, 0)

    wide = math.gcd(piece, 256)

    def pull(place, c, store):
        def step(i, carry):
            lanes = pl.ds(pl.multiple_of(c * piece + i * wide, wide), wide)
            store(
                lanes,
                lax.dot_general(
                    out_ref[place],
                    weight_ref[lanes, :],
                    (((1,), (1,)), ((), ())),
                    preferred_element_type=f32,
                ),
            )
            return carry

        lax.fori_loop(0, piece // wide, step, 0)

    def to_send(slot):
        def store(lanes, value):
            send_ref[slot, :, lanes] = value.astype(bf16)

        return store

    def to_hold(lanes, value):
        hold_ref[:, lanes] = value

    parts = [
        [
            remote(
                "dp",
                send_ref.at[n, :, span_of(c)],
                land_ref.at[n, :, span_of(c)],
                part_send.at[n, c],
                part_recv.at[n, c],
                across if n == 1 else sibling,
            )
            for c in range(pieces)
        ]
        for n in range(3)
    ]

    def join(c):
        parts[0][c].wait_recv()

        def step(first):
            lanes = lanes_at(first)
            send_ref[1, :, lanes] = (
                hold_ref[:, lanes] + land_ref[0, :, lanes].astype(f32)
            ).astype(bf16)

        piece_loop(c, step)
        parts[1][c].start()

    slopes(3)
    slopes(2)
    for c in range(pieces):
        pull(3, c, to_send(0))
        parts[0][c].start()
        pull(2, c, to_hold)
        if c > 0:
            join(c - 1)
    join(pieces - 1)
    slopes(1)
    for c in range(pieces):
        pull(1, c, to_send(2))
        parts[2][c].start()
    slopes(0)
    for c in range(pieces):
        pull(0, c, to_hold)

    def conv_slopes(first):
        lanes = lanes_at(first)
        total = (
            hold_ref[:, lanes]
            + land_ref[2, :, lanes].astype(f32)
            + land_ref[1, :, lanes].astype(f32)
        )
        values = []
        for s in range(2):
            own = total[s * rows : (s + 1) * rows]
            slope_ref[s, :, lanes] = own * conv_ref[s, :, lanes].astype(f32)
            values.append((own * query_ref[s, :, lanes].astype(f32)).astype(bf16).astype(f32))
            local_ref[s, :, lanes] = values[s]

        def store(s, m, value):
            back_going_ref[s, pl.ds(m, 1), lanes] = value

        block_states(values, rate_ref[:, lanes], False, store)

    def back_direct(first):
        lanes = lanes_at(first)
        for s in range(2):
            local_ref[s, :, lanes] = direct_conv(
                local_ref[s, :, lanes], lambda j: table_ref[pl.ds(j, 1), lanes], False
            )

    def backward_pass(c):
        for n in range(c * links_each, (c + 1) * links_each):
            pass_on(
                n, back_going_ref, back_coming_ref, backward_chain, at_end, inside_end, inside_start
            )

    def tapped(unit, lanes, next_one, next_two):
        high = unit.shape[0]
        row = lax.broadcasted_iota(jnp.int32, unit.shape, 0)
        one = jnp.where(row < high - 1, pltpu.roll(unit, high - 1, 0), next_one)
        two = jnp.where(
            row < high - 2,
            pltpu.roll(unit, high - 2, 0),
            jnp.where(row == high - 2, next_one, next_two),
        )
        return (
            tap_ref[0:1, lanes] * unit + tap_ref[1:2, lanes] * one + tap_ref[2:3, lanes] * two
        ).astype(bf16)

    def units(first):
        places = [lanes_at(first + j * width) for j in range(3)]
        lanes = places[0]
        full = reached(
            [local_ref[s, :, lanes] for s in range(2)],
            lambda s, m: back_coming_ref[s, pl.ds(m, 1), lanes],
            res_ref[:, lanes],
            rate_ref[:, lanes],
            False,
        )
        none = jnp.zeros((1, LANES), f32)
        for j, place in enumerate(places):
            firsts = []
            for s in range(2):
                if j == 0:
                    unit = slope_ref[s, :, lanes]
                else:
                    other = value_ref if j == 1 else key_ref
                    unit = full[s].astype(bf16).astype(f32) * other[s, :, lanes]
                firsts.append(unit[:2])
                tail_ref[s, :, place] = unit[rows - 16 :]
                grads[s][0, :, place] = tapped(unit, place, none, none)
            head_out[:, place] = jnp.concatenate(firsts + [jnp.zeros((4, LANES), f32)], 0)

    def arrive(c):
        parts[2][c].wait_recv()
        parts[1][c].wait_recv()
        piece_loop(c, conv_slopes)

    @pl.when(upper)
    def _():
        for c in range(pieces):
            arrive(c)
            backward_pass(c)
        for c in range(pieces):
            piece_loop(c, back_direct)
            piece_loop(c, units)

    @pl.when(lower)
    def _():
        for c in range(pieces):
            arrive(c)
            piece_loop(c, back_direct)
        for c in range(pieces):
            backward_pass(c)
            piece_loop(c, units)

    head = remote("ctx", head_out, head_in, head_sem.at[0], head_sem.at[1], before)

    @pl.when(inside_start)
    def _():
        head.start()

    @pl.when(inside_end)
    def _():
        head.wait_recv()

        def mend(lanes):
            for s in range(2):
                grads[s][0, rows - 16 :, lanes] = tapped(
                    tail_ref[s, :, lanes],
                    lanes,
                    head_in[2 * s : 2 * s + 1, lanes],
                    head_in[2 * s + 1 : 2 * s + 2, lanes],
                )

        lane_loop(3 * width, mend)

    for group in row_copies + parts:
        for one in group:
            one.wait_send()

    @pl.when(inside_end)
    def _():
        halo.wait_send()
        for one in forward_chain:
            one.wait_send()

    @pl.when(inside_start)
    def _():
        head.wait_send()
        for one in backward_chain:
            one.wait_send()


def mixer_grads(feats, taps, res, rate, gain, weight):
    _, rows, width3 = feats[0].shape
    width, modes, own_width = width3 // 3, res.shape[0], weight.shape[1]
    pieces, links = math.gcd(width // LANES, 4), math.gcd(width // LANES, 16)
    vmem = pl.BlockSpec(memory_space=pltpu.VMEM)
    dma = pltpu.SemaphoreType.DMA
    return pl.pallas_call(
        mixer_grads_kernel,
        in_specs=[vmem] * 7 + [pl.BlockSpec(memory_space=pl.ANY)],
        out_specs=[vmem] * 2,
        out_shape=[jax.ShapeDtypeStruct((1, rows, width3), bf16)] * 2,
        scratch_shapes=[
            pltpu.VMEM(weight.shape, bf16),
            pltpu.VMEM((3, rows, width), bf16),
            pltpu.VMEM((2, rows, width), f32),
            pltpu.VMEM((2, rows, width), f32),
            pltpu.VMEM((2, rows, width), bf16),
            pltpu.VMEM((3 * rows, width), bf16),
            pltpu.VMEM((rows, width), f32),
            pltpu.VMEM((3, rows, width), f32),
            pltpu.VMEM((2, rows, width), f32),
            pltpu.VMEM((2, rows, width), f32),
            pltpu.VMEM((2, 16, width3), f32),
            pltpu.VMEM((SUB, width3), f32),
            pltpu.VMEM((SUB, width3), f32),
            pltpu.VMEM((SUB, width3), f32),
            pltpu.VMEM((SUB, width3), f32),
            pltpu.VMEM((3, modes, width), f32),
            pltpu.VMEM((3, modes, width), f32),
            pltpu.VMEM((2, modes, width), f32),
            pltpu.VMEM((2, modes, width), f32),
            pltpu.VMEM((3, 3 * rows, width), bf16),
            pltpu.VMEM((4, 3 * rows, own_width), f32),
            pltpu.VMEM((4 * rows, LANES), f32),
            pltpu.VMEM((4, 4, SUB, rows), f32),
            pltpu.VMEM((4, 2 * rows, own_width), bf16),
            pltpu.VMEM((2 * rows, width), f32),
            pltpu.VMEM((3, 2 * rows, width), bf16),
            pltpu.VMEM((3, 2 * rows, width), bf16),
            dma((1,)),
            dma((2,)),
            dma((2,)),
            dma((links,)),
            dma((links,)),
            dma((links,)),
            dma((links,)),
            dma((3, pieces)),
            dma((3, pieces)),
            dma((3,)),
            dma((3,)),
            dma((3, pieces)),
            dma((3, pieces)),
        ],
        compiler_params=pltpu.CompilerParams(
            collective_id=0, has_side_effects=True, vmem_limit_bytes=60 * 2**20
        ),
        name="mixer_grads",
    )(*feats, taps, res, rate, gain, weight)


def per_device(
    feat_clean, feat_pert, feat_teacher, short_taps, residues, decay_rate, out_weight, norm_gain
):
    own_width = out_weight.shape[1]
    gain = lax.dynamic_slice_in_dim(norm_gain, lax.axis_index("dp") * own_width, own_width, 0)
    return mixer_grads(
        (feat_clean, feat_pert, feat_teacher),
        short_taps,
        residues.T,
        decay_rate.T,
        gain[None],
        out_weight,
    )


def solution(mesh):
    in_specs = (
        P("dp", "ctx", None),
        P("dp", "ctx", None),
        P("dp", "ctx", None),
        P(),
        P(),
        P(),
        P(None, "dp"),
        P(),
    )
    out_specs = (P("dp", "ctx", None), P("dp", "ctx", None))
    return jax.shard_map(
        per_device, mesh=mesh, in_specs=in_specs, out_specs=out_specs, check_vma=False
    )
```
